32 devices in a mesh: dp: 4 (over y, x), expert: 8 (over z, core).
Axes of the slice: x: 2, y: 2, z: 4, core: 2. Of those that a mesh axis runs over, the one named last changes fastest.
Arguments:
- out_grad: bfloat16 [4, 1024, 4096], P('dp', 'expert'), may hold values from -6 to 6
- count: int32 [4, 1024], P('dp', 'expert'), may hold values from 0 to 8, as said below
- chosen: int32 [4, 16, 128], P('dp', 'expert'), may hold values from 0 to 1023, as said below
- gates: float32 [4, 16, 128], P('dp', 'expert'), may hold values from 0.1 to 1
- x_slots: bfloat16 [4, 16, 128, 4096], P('dp', 'expert'), may hold values from -6 to 6
- w_in: bfloat16 [16, 4096, 512], P('expert', None, 'dp'), may hold values from -0.09375 to 0.09375
- w_out: bfloat16 [16, 512, 4096], P('expert', 'dp'), may hold values from -0.25 to 0.25
Outputs:
- token_grad: bfloat16 [4, 1024, 4096], P('dp', 'expert')
- gate_grad: float32 [4, 16, 128], P('dp', 'expert')
- w_in_grad: bfloat16 [16, 4096, 512], P('expert', None, 'dp')
- w_out_grad: bfloat16 [16, 512, 4096], P('expert', 'dp')
The draws below stay inside these ranges and needn't reach their ends.
Inputs may be any that keep to these rules, and one draw needn't show every extreme that they name: `chosen`: in each group, one expert's 128 slots name different tokens, and one device's 2 experts together name different tokens. Within a group, the slots of one device's experts name at most 48 tokens of any one device (device j of expert holds the group's tokens j * 128 to (j + 1) * 128 - 1), and every such device's experts name exactly 48 tokens of some device. count[g,t] is the number of slots of group g, over all experts, whose chosen token is t; each device of expert contributes at most one.
All inputs are finite; a program needn't handle non-finite values.
Results may differ from the reference program's by a relative error of at most 0.007.
Values may be sent and summed in bfloat16 or wider, within the bound.
A program may use at most 128 MiB of HBM per device.

```python
import math
import jax
import jax.numpy as jnp
from jax import lax

D = 4096
FF = 512
EXP_DEV = 2
TOK_DEV = 128
EXPERTS = 16
TOK_GROUP = 1024
CAP = 128
PEER = 48
N_DP = 4
N_EXPERT = 8


def route_tables(key):
    slots = EXP_DEV * CAP
    key_shared, key_owners = jax.random.split(key)
    shared_rows = jax.random.randint(key_shared, (N_DP, N_EXPERT), 0, TOK_DEV)
    owner_keys = jax.random.split(key_owners, N_DP * N_EXPERT)
    group_of_owner = jnp.arange(N_DP * N_EXPERT, dtype=jnp.int32) // N_EXPERT

    def one_owner(owner_key, group_index):
        key_order, key_offset, key_shuffle = jax.random.split(owner_key, 3)
        source_order = jax.random.permutation(key_order, N_EXPERT)
        hot_source = source_order[0]
        cold_sources = source_order[1:]
        slot_ids = jnp.arange(slots, dtype=jnp.int32)
        later = jnp.maximum(slot_ids - PEER, 0)
        source = jnp.where(slot_ids < PEER, hot_source, cold_sources[later % (N_EXPERT - 1)])
        slot_rank = jnp.where(slot_ids < PEER, slot_ids, later // (N_EXPERT - 1))
        offsets = jax.random.randint(key_offset, (N_EXPERT,), 0, TOK_DEV - 1)
        base_row = shared_rows[group_index][source]
        step_row = (jnp.maximum(slot_rank - 1, 0) + offsets[source]) % (TOK_DEV - 1) + 1
        local_row = jnp.where(slot_rank == 0, base_row, (base_row + step_row) % TOK_DEV)
        token_ids = source * TOK_DEV + local_row
        shuffle = jax.random.permutation(key_shuffle, slots)
        return token_ids[shuffle].reshape(EXP_DEV, CAP)
    tables = jax.vmap(one_owner)(owner_keys, group_of_owner)
    return tables.reshape(N_DP, N_EXPERT * EXP_DEV, CAP).astype(jnp.int32)


def token_counts(tables):
    group_ids = jnp.broadcast_to(jnp.arange(N_DP, dtype=jnp.int32)[:, None, None], tables.shape)
    totals = jnp.zeros((N_DP, TOK_GROUP), jnp.int32)
    return totals.at[group_ids.reshape(-1), tables.reshape(-1)].add(1)


def draw_chosen(key, part):
    tables = route_tables(key)
    return tables


def draw_count(key, part):
    tables = route_tables(key)
    return token_counts(tables)


def draw_out_grad(key, part):
    totals = token_counts(route_tables(key))
    key = jax.random.fold_in(key, 7)
    key_base, key_size = jax.random.split(key)
    shape = (N_DP, TOK_GROUP, D)
    base = jax.random.truncated_normal(key_base, -6.0, 6.0, shape, jnp.float32)
    magnitude = jax.random.uniform(key_size, shape, jnp.float32, 3.0, 6.0)
    strong = jnp.where(base >= 0.0, magnitude, -magnitude)
    popular = (2 * totals >= N_EXPERT)[:, :, None]
    return jnp.where(popular, strong, base).astype(jnp.bfloat16)


def block_scale(key, dims, cuts, low, top_value):
    level = 1.0
    for position, blocks in cuts:
        heights = jax.random.uniform(jax.random.fold_in(jax.random.fold_in(key, 6), position), (blocks,), jnp.float32, low / len(cuts), top_value / len(cuts))
        level = level * jnp.repeat(jnp.exp(heights), dims[position] // blocks).reshape((-1,) + (1,) * (len(dims) - 1 - position))
    return level


def scatter_about(rng, extent, scale, limit, pieces=(), kind=jnp.bfloat16):
    entries = scale * jax.random.normal(rng, extent, jnp.float32)
    if pieces:
        entries = entries * block_scale(rng, extent, pieces, -0.22, 0.18)
    return jnp.clip(entries, -limit, limit).astype(kind)


def setup_inputs(seed: int = 0) -> dict:
    splits = jax.random.split(jax.random.key(seed), 8)
    out_grad = draw_out_grad(jax.random.fold_in(splits[7], 71), 0)
    count = draw_count(jax.random.fold_in(splits[7], 71), 0)
    chosen = draw_chosen(jax.random.fold_in(splits[7], 71), 0)
    gates = jnp.clip(jnp.exp(math.log(1.0) - 2.3025851 * jax.random.uniform(splits[3], (N_DP, EXPERTS, CAP), jnp.float32) ** block_scale(splits[3], (N_DP, EXPERTS, CAP), ((0, 4), (1, 8)), -0.2, 0.2)), 0.1, 1.0)
    x_slots = scatter_about(splits[4], (N_DP, EXPERTS, CAP, D), 1.0, 6.0, ((0, 4), (1, 8)))
    w_in = scatter_about(splits[5], (EXPERTS, D, FF), D ** -0.5, 0.09375, ((0, 8), (2, 4)))
    w_out = scatter_about(splits[6], (EXPERTS, FF, D), FF ** -0.5, 0.25, ((0, 8), (1, 4)))
    return {"out_grad": out_grad, "count": count, "chosen": chosen, "gates": gates, "x_slots": x_slots, "w_in": w_in, "w_out": w_out}


SQRT_HALF = 0.7071067811865476
INV_ROOT_TWO_PI = 0.3989422804014327


def activation(pre):
    normal_cdf = 0.5 * (1.0 + lax.erf(pre * SQRT_HALF))
    slope = normal_cdf + pre * jnp.exp(-0.5 * pre * pre) * INV_ROOT_TWO_PI
    return pre * normal_cdf, slope


def pick_rows(table, token_ids):
    return table[token_ids]


def reference(out_grad, count, chosen, gates, x_slots, w_in, w_out):
    groups = out_grad.shape[0]
    width = out_grad.shape[2]

    def per_expert(items):
        token_ids, gate_e, inputs, proj_in, proj_out = items
        upstream = jax.vmap(pick_rows)(out_grad, token_ids)
        slot_count = jax.vmap(pick_rows)(count, token_ids).astype(jnp.float32).reshape(-1)
        scale_flat = gate_e.reshape(-1) / slot_count
        rows_per = inputs.shape[1]
        flat_in = inputs.reshape(-1, width)
        flat_up = upstream.reshape(-1, width)
        pre = jnp.dot(flat_in, proj_in, preferred_element_type=jnp.float32)
        hidden_f, slope = activation(pre)
        hidden = hidden_f.astype(jnp.bfloat16)
        project = jnp.dot(flat_up, proj_out.T, preferred_element_type=jnp.float32)
        gate_part = jnp.sum(hidden.astype(jnp.float32) * project, axis=1) / slot_count
        pre_grad = (scale_flat[:, None] * project * slope).astype(jnp.bfloat16)
        out_slot = (scale_flat[:, None] * flat_up.astype(jnp.float32)).astype(jnp.bfloat16)
        back_part = jnp.dot(pre_grad, proj_in.T, preferred_element_type=jnp.float32).astype(jnp.bfloat16)
        grad_in = jnp.zeros(proj_in.shape, jnp.float32)
        grad_out = jnp.zeros(proj_out.shape, jnp.float32)
        for group in range(groups):
            low = group * rows_per
            high = low + rows_per
            term_in = jnp.dot(flat_in[low:high].T, pre_grad[low:high], preferred_element_type=jnp.float32)
            term_out = jnp.dot(hidden[low:high].T, out_slot[low:high], preferred_element_type=jnp.float32)
            grad_in = grad_in + lax.optimization_barrier(term_in.astype(jnp.bfloat16)).astype(jnp.float32)
            grad_out = grad_out + lax.optimization_barrier(term_out.astype(jnp.bfloat16)).astype(jnp.float32)
        return (back_part.reshape(groups, rows_per, width), gate_part.reshape(groups, rows_per),
                grad_in.astype(jnp.bfloat16), grad_out.astype(jnp.bfloat16))

    back_all, gate_all, w_in_grad, w_out_grad = lax.map(
        per_expert,
        (jnp.swapaxes(chosen, 0, 1), jnp.swapaxes(gates, 0, 1), jnp.swapaxes(x_slots, 0, 1), w_in, w_out))
    token_grad = jnp.zeros((groups, count.shape[1], width), jnp.float32)
    for group in range(groups):
        token_grad = token_grad.at[group, chosen[group].reshape(-1)].add(
            back_all[:, group].reshape(-1, width).astype(jnp.float32))
    return token_grad.astype(jnp.bfloat16), jnp.swapaxes(gate_all, 0, 1), w_in_grad, w_out_grad
```

```python
import jax
import jax.numpy as jnp
from jax import lax
from jax.sharding import PartitionSpec as P

SQRT_HALF = 0.7071067811865476
INV_ROOT_TWO_PI = 0.3989422804014327
BF16 = jnp.bfloat16
F32 = jnp.float32


def swap(value, bit):
    size = lax.axis_size("dp")
    return lax.ppermute(value, "dp", [(i, i ^ bit) for i in range(size)])


def running_rank(mask):
    n = mask.shape[-1]
    before = (jnp.arange(n)[:, None] < jnp.arange(n)[None, :]).astype(BF16)
    ranks = jnp.dot(mask.astype(BF16), before, preferred_element_type=F32)
    return ranks.astype(jnp.int32)


def shards(out_grad, count, chosen, gates, x_slots, w_in, w_out):
    tok_rows, width = out_grad.shape[1:]
    experts, cap = chosen.shape[1:]
    slots = experts * cap
    owners = lax.axis_size("expert")
    per_peer = 3 * tok_rows // owners
    places = owners * per_peer
    me = lax.axis_index("expert")

    x_own = x_slots[0]
    w_in_other = swap(w_in, 1)
    x_other = swap(x_own, 2)
    w_out_other = swap(w_out, 1)

    tokens = chosen.reshape(slots)
    table = lax.all_gather(jnp.concatenate([tokens, count[0]]), "expert", axis=0)
    all_tokens, all_counts = table[:, :slots], table[:, slots:].reshape(-1)

    asked = all_tokens // tok_rows == me
    rank = running_rank(asked)
    local = all_tokens % tok_rows
    place = jnp.where(asked, rank, per_peer)
    picks = place[:, None, :] == jnp.arange(per_peer)[None, :, None]
    row_of = jnp.sum(jnp.where(picks, local[:, None, :] + 1, 0), axis=2).reshape(places) - 1
    send_pick = (row_of[:, None] == jnp.arange(tok_rows)[None, :]).astype(BF16)
    sent = jnp.dot(send_pick, out_grad[0], preferred_element_type=F32).astype(BF16)
    got = lax.all_to_all(
        sent.reshape(owners, per_peer, width), "expert", split_axis=0, concat_axis=0, tiled=True
    ).reshape(places, width)

    source = tokens // tok_rows
    from_source = source[None, :] == jnp.arange(owners)[:, None]
    slot_rank = jnp.sum(jnp.where(from_source, running_rank(from_source), 0), axis=0)
    slot_place = source * per_peer + slot_rank
    slot_pick = (slot_place[:, None] == jnp.arange(places)[None, :]).astype(BF16)
    slot_grad = jnp.dot(slot_pick, got, preferred_element_type=F32).astype(BF16)
    slot_count = jnp.sum(
        jnp.where(tokens[:, None] == jnp.arange(owners * tok_rows)[None, :], all_counts[None, :], 0),
        axis=1,
    ).astype(F32)
    slot_scale = gates.reshape(slots) / slot_count
    own_scalars = jnp.stack([slot_scale, slot_count]).reshape(2, experts, cap)
    grad_own = slot_grad.reshape(experts, cap, width)
    other_scalars = swap(own_scalars, 2)
    grad_other = swap(grad_own, 2)

    inputs = jnp.concatenate([x_own, x_other], axis=1)
    proj_in = jnp.concatenate([w_in, w_in_other], axis=2)
    proj_out = jnp.concatenate([w_out, w_out_other], axis=1)
    upstream = jnp.concatenate([grad_own, grad_other], axis=1)
    scale, counts = jnp.concatenate([own_scalars, other_scalars], axis=2)

    pre = jnp.einsum("ecd,edf->ecf", inputs, proj_in, preferred_element_type=F32)
    normal_cdf = 0.5 * (1.0 + lax.erf(pre * SQRT_HALF))
    slope = normal_cdf + pre * jnp.exp(-0.5 * pre * pre) * INV_ROOT_TWO_PI
    hidden = (pre * normal_cdf).astype(BF16)

    out_slot = (scale[..., None] * upstream.astype(F32)).astype(BF16)
    quarter = w_in.shape[2]
    grad_out_other = jnp.einsum(
        "ecf,ecd->efd", hidden[..., quarter:], out_slot, preferred_element_type=F32
    ).astype(BF16)
    grad_out_got = swap(grad_out_other, 1)

    project = jnp.einsum("ecd,efd->ecf", upstream, proj_out, preferred_element_type=F32)
    gate_part = jnp.sum(hidden.astype(F32) * project, axis=2) / counts
    pre_grad = (scale[..., None] * project * slope).astype(BF16)
    back_other = jnp.einsum(
        "ecf,edf->ecd", pre_grad[:, cap:], proj_in, preferred_element_type=F32
    ).astype(BF16)
    back_got = swap(back_other, 2)
    gate_got = swap(gate_part[:, cap:], 2)
    grad_in_other = jnp.einsum(
        "ecd,ecf->edf", inputs, pre_grad[..., quarter:], preferred_element_type=F32
    ).astype(BF16)
    grad_in_got = swap(grad_in_other, 1)

    back_own = jnp.einsum("ecf,edf->ecd", pre_grad[:, :cap], proj_in, preferred_element_type=F32)
    slot_back = (back_own + back_got.astype(F32)).astype(BF16).reshape(slots, width)
    outgoing = jnp.dot(slot_pick.T, slot_back, preferred_element_type=F32).astype(BF16)
    returned = lax.all_to_all(
        outgoing.reshape(owners, per_peer, width), "expert", split_axis=0, concat_axis=0, tiled=True
    ).reshape(places, width)

    grad_out_own = jnp.einsum(
        "ecf,ecd->efd", hidden[..., :quarter], out_slot, preferred_element_type=F32
    )
    w_out_grad = (grad_out_own + grad_out_got.astype(F32)).astype(BF16)
    grad_in_own = jnp.einsum(
        "ecd,ecf->edf", inputs, pre_grad[..., :quarter], preferred_element_type=F32
    )
    w_in_grad = (grad_in_own + grad_in_got.astype(F32)).astype(BF16)
    token_grad = jnp.dot(send_pick.T, returned, preferred_element_type=F32).astype(BF16)
    gate_grad = gate_part[:, :cap] + gate_got
    return token_grad[None], gate_grad[None], w_in_grad, w_out_grad


def solution(mesh):
    return jax.shard_map(
        shards,
        mesh=mesh,
        in_specs=(
            P("dp", "expert", None),
            P("dp", "expert"),
            P("dp", "expert", None),
            P("dp", "expert", None),
            P("dp", "expert", None, None),
            P("expert", None, "dp"),
            P("expert", "dp", None),
        ),
        out_specs=(
            P("dp", "expert", None),
            P("dp", "expert", None),
            P("expert", None, "dp"),
            P("expert", "dp", None),
        ),
        check_vma=False,
    )
```

```python
import jax
import jax.numpy as jnp
from jax import lax
from jax.sharding import PartitionSpec as P

SQRT_HALF = 0.7071067811865476
INV_ROOT_TWO_PI = 0.3989422804014327
BF16 = jnp.bfloat16
F32 = jnp.float32
PARTS = 2


def swap(value, bit):
    size = lax.axis_size("dp")
    return lax.ppermute(value, "dp", [(i, i ^ bit) for i in range(size)])


def exchange(rows, owners):
    blocks = rows.reshape(owners, -1, rows.shape[1])
    got = lax.all_to_all(blocks, "expert", split_axis=0, concat_axis=0, tiled=True)
    return got.reshape(rows.shape)


def running_rank(mask):
    n = mask.shape[-1]
    before = (jnp.arange(n)[:, None] < jnp.arange(n)[None, :]).astype(BF16)
    ranks = jnp.dot(mask.astype(BF16), before, preferred_element_type=F32)
    return ranks.astype(jnp.int32)


def shards(out_grad, count, chosen, gates, x_slots, w_in, w_out):
    tok_rows, width = out_grad.shape[1:]
    experts, cap = chosen.shape[1:]
    slots = experts * cap
    owners = lax.axis_size("expert")
    per_peer = 3 * tok_rows // owners
    places = owners * per_peer
    me = lax.axis_index("expert")

    x_own = x_slots[0]
    w_in_other = swap(w_in, 1)
    x_other = swap(x_own, 2)
    w_out_other = swap(w_out, 1)

    tokens = chosen.reshape(slots)
    table = lax.all_gather(jnp.concatenate([tokens, count[0]]), "expert", axis=0)
    all_tokens, all_counts = table[:, :slots], table[:, slots:].reshape(-1)

    asked = all_tokens // tok_rows == me
    rank = running_rank(asked)
    local = all_tokens % tok_rows
    place = jnp.where(asked, rank, per_peer)
    picks = place[:, None, :] == jnp.arange(per_peer)[None, :, None]
    row_of = jnp.sum(jnp.where(picks, local[:, None, :] + 1, 0), axis=2).reshape(places) - 1
    send_pick = (row_of[:, None] == jnp.arange(tok_rows)[None, :]).astype(BF16)

    source = tokens // tok_rows
    from_source = source[None, :] == jnp.arange(owners)[:, None]
    slot_rank = jnp.sum(jnp.where(from_source, running_rank(from_source), 0), axis=0)
    slot_place = source * per_peer + slot_rank
    slot_pick = (slot_place[:, None] == jnp.arange(places)[None, :]).astype(BF16)
    slot_count = jnp.sum(
        jnp.where(tokens[:, None] == jnp.arange(owners * tok_rows)[None, :], all_counts[None, :], 0),
        axis=1,
    ).astype(F32)
    slot_scale = gates.reshape(slots) / slot_count
    own_scalars = jnp.stack([slot_scale, slot_count]).reshape(2, experts, cap)
    other_scalars = swap(own_scalars, 2)

    part = width // PARTS
    columns = [slice(k * part, (k + 1) * part) for k in range(PARTS)]
    upstream = []
    for cols in columns:
        sent = jnp.dot(send_pick, out_grad[0][:, cols], preferred_element_type=F32).astype(BF16)
        got = exchange(sent, owners)
        grad_own = jnp.dot(slot_pick, got, preferred_element_type=F32).astype(BF16)
        grad_own = grad_own.reshape(experts, cap, part)
        upstream.append(jnp.concatenate([grad_own, swap(grad_own, 2)], axis=1))

    inputs = jnp.concatenate([x_own, x_other], axis=1)
    proj_in = jnp.concatenate([w_in, w_in_other], axis=2)
    proj_out = jnp.concatenate([w_out, w_out_other], axis=1)
    scale, counts = jnp.concatenate([own_scalars, other_scalars], axis=2)

    pre = jnp.einsum("ecd,edf->ecf", inputs, proj_in, preferred_element_type=F32)
    normal_cdf = 0.5 * (1.0 + lax.erf(pre * SQRT_HALF))
    slope = normal_cdf + pre * jnp.exp(-0.5 * pre * pre) * INV_ROOT_TWO_PI
    hidden = (pre * normal_cdf).astype(BF16)

    out_slot = [(scale[..., None] * u.astype(F32)).astype(BF16) for u in upstream]
    quarter = w_in.shape[2]
    project = sum(
        jnp.einsum("ecd,efd->ecf", u, proj_out[..., cols], preferred_element_type=F32)
        for u, cols in zip(upstream, columns)
    )
    gate_part = jnp.sum(hidden.astype(F32) * project, axis=2) / counts
    pre_grad = (scale[..., None] * project * slope).astype(BF16)
    gate_got = swap(gate_part[:, cap:], 2)

    def grad_out(units):
        terms = [jnp.einsum("ecf,ecd->efd", units, o, preferred_element_type=F32) for o in out_slot]
        return jnp.concatenate(terms, axis=2)

    def grad_in(units):
        return jnp.einsum("ecd,ecf->edf", inputs, units, preferred_element_type=F32)

    back_got = []
    for k, cols in enumerate(columns):
        back_other = jnp.einsum(
            "ecf,edf->ecd", pre_grad[:, cap:], proj_in[:, cols], preferred_element_type=F32
        ).astype(BF16)
        if k == 0:
            grad_out_other = grad_out(hidden[..., quarter:]).astype(BF16)
            back_other, grad_out_other = lax.optimization_barrier((back_other, grad_out_other))
            grad_out_got = swap(grad_out_other, 1)
        if k == PARTS - 1:
            grad_in_other = grad_in(pre_grad[..., quarter:]).astype(BF16)
            back_other, grad_in_other = lax.optimization_barrier((back_other, grad_in_other))
            grad_in_got = swap(grad_in_other, 1)
        back_got.append(swap(back_other, 2))

    returned = []
    for k, cols in enumerate(columns):
        back_own = jnp.einsum(
            "ecf,edf->ecd", pre_grad[:, :cap], proj_in[:, cols], preferred_element_type=F32
        )
        slot_back = (back_own + back_got[k].astype(F32)).astype(BF16).reshape(slots, part)
        outgoing = jnp.dot(slot_pick.T, slot_back, preferred_element_type=F32).astype(BF16)
        if k == PARTS - 1:
            outgoing, grad_out_got = lax.optimization_barrier((outgoing, grad_out_got))
        returned.append(exchange(outgoing, owners))

    w_out_grad = (grad_out(hidden[..., :quarter]) + grad_out_got.astype(F32)).astype(BF16)
    returned[-1], grad_in_got = lax.optimization_barrier((returned[-1], grad_in_got))
    w_in_grad = (grad_in(pre_grad[..., :quarter]) + grad_in_got.astype(F32)).astype(BF16)
    token_grad = jnp.concatenate(
        [jnp.dot(send_pick.T, r, preferred_element_type=F32).astype(BF16) for r in returned], axis=1
    )
    gate_grad = gate_part[:, :cap] + gate_got
    return token_grad[None], gate_grad[None], w_in_grad, w_out_grad


def solution(mesh):
    return jax.shard_map(
        shards,
        mesh=mesh,
        in_specs=(
            P("dp", "expert", None),
            P("dp", "expert"),
            P("dp", "expert", None),
            P("dp", "expert", None),
            P("dp", "expert", None, None),
            P("expert", None, "dp"),
            P("expert", "dp", None),
        ),
        out_specs=(
            P("dp", "expert", None),
            P("dp", "expert", None),
            P("expert", None, "dp"),
            P("expert", "dp", None),
        ),
        check_vma=False,
    )
```

```python
import jax
import jax.numpy as jnp
from jax import lax
from jax.sharding import PartitionSpec as P

SQRT_HALF = 0.7071067811865476
INV_ROOT_TWO_PI = 0.3989422804014327
BF16 = jnp.bfloat16
F32 = jnp.float32
PARTS = 2


def swap(value, bit):
    size = lax.axis_size("dp")
    return lax.ppermute(value, "dp", [(i, i ^ bit) for i in range(size)])


def exchange(rows, owners):
    blocks = rows.reshape(owners, -1, rows.shape[1])
    got = lax.all_to_all(blocks, "expert", split_axis=0, concat_axis=0, tiled=True)
    return got.reshape(rows.shape)


def running_rank(mask):
    n = mask.shape[-1]
    before = (jnp.arange(n)[:, None] < jnp.arange(n)[None, :]).astype(BF16)
    ranks = jnp.dot(mask.astype(BF16), before, preferred_element_type=F32)
    return ranks.astype(jnp.int32)


def shards(out_grad, count, chosen, gates, x_slots, w_in, w_out):
    tok_rows, width = out_grad.shape[1:]
    experts, cap = chosen.shape[1:]
    slots = experts * cap
    owners = lax.axis_size("expert")
    per_peer = 3 * tok_rows // owners
    places = owners * per_peer
    me = lax.axis_index("expert")

    x_own = x_slots[0]
    w_in_other = swap(w_in, 1)
    x_other = swap(x_own, 2)
    w_out_other = swap(w_out, 1)

    tokens = chosen.reshape(slots)
    table = lax.all_gather(jnp.concatenate([tokens, count[0]]), "expert", axis=0)
    all_tokens, all_counts = table[:, :slots], table[:, slots:].reshape(-1)

    asked = all_tokens // tok_rows == me
    rank = running_rank(asked)
    local = all_tokens % tok_rows
    place = jnp.where(asked, rank, per_peer)
    picks = place[:, None, :] == jnp.arange(per_peer)[None, :, None]
    row_of = jnp.sum(jnp.where(picks, local[:, None, :] + 1, 0), axis=2).reshape(places) - 1
    send_pick = (row_of[:, None] == jnp.arange(tok_rows)[None, :]).astype(BF16)

    source = tokens // tok_rows
    from_source = source[None, :] == jnp.arange(owners)[:, None]
    slot_rank = jnp.sum(jnp.where(from_source, running_rank(from_source), 0), axis=0)
    slot_place = source * per_peer + slot_rank
    slot_pick = (slot_place[:, None] == jnp.arange(places)[None, :]).astype(BF16)
    slot_count = jnp.sum(
        jnp.where(tokens[:, None] == jnp.arange(owners * tok_rows)[None, :], all_counts[None, :], 0),
        axis=1,
    ).astype(F32)
    slot_scale = gates.reshape(slots) / slot_count
    own_scalars = jnp.stack([slot_scale, slot_count]).reshape(2, experts, cap)
    other_scalars = swap(own_scalars, 2)

    part = width // PARTS
    columns = [slice(k * part, (k + 1) * part) for k in range(PARTS)]
    upstream = []
    for k, cols in enumerate(columns):
        sent = jnp.dot(send_pick, out_grad[0][:, cols], preferred_element_type=F32).astype(BF16)
        if k == 1:
            sent, x_other, w_in_other = lax.optimization_barrier((sent, x_other, w_in_other))
        got = exchange(sent, owners)
        grad_own = jnp.dot(slot_pick, got, preferred_element_type=F32).astype(BF16)
        grad_own = grad_own.reshape(experts, cap, part)
        grad_other = swap(grad_own, 2)
        if k == PARTS - 1:
            grad_other, other_scalars = lax.optimization_barrier((grad_other, other_scalars))
        upstream.append(jnp.concatenate([grad_own, grad_other], axis=1))

    inputs = jnp.concatenate([x_own, x_other], axis=1)
    proj_in = jnp.concatenate([w_in, w_in_other], axis=2)
    proj_out = jnp.concatenate([w_out, w_out_other], axis=1)
    scale, counts = jnp.concatenate([own_scalars, other_scalars], axis=2)

    pre = jnp.einsum("ecd,edf->ecf", inputs, proj_in, preferred_element_type=F32)
    normal_cdf = 0.5 * (1.0 + lax.erf(pre * SQRT_HALF))
    slope = normal_cdf + pre * jnp.exp(-0.5 * pre * pre) * INV_ROOT_TWO_PI
    hidden = (pre * normal_cdf).astype(BF16)

    out_slot = [(scale[..., None] * u.astype(F32)).astype(BF16) for u in upstream]
    quarter = w_in.shape[2]
    project = sum(
        jnp.einsum("ecd,efd->ecf", u, proj_out[..., cols], preferred_element_type=F32)
        for u, cols in zip(upstream, columns)
    )
    gate_part = jnp.sum(hidden.astype(F32) * project, axis=2) / counts
    pre_grad = (scale[..., None] * project * slope).astype(BF16)
    gate_got = swap(gate_part[:, cap:], 2)

    def grad_out(units):
        terms = [jnp.einsum("ecf,ecd->efd", units, o, preferred_element_type=F32) for o in out_slot]
        return jnp.concatenate(terms, axis=2)

    def grad_in(units):
        return jnp.einsum("ecd,ecf->edf", inputs, units, preferred_element_type=F32)

    grad_out_other = grad_out(hidden[..., quarter:]).astype(BF16)
    back_other = jnp.einsum(
        "ecf,edf->ecd", pre_grad[:, cap:], proj_in, preferred_element_type=F32
    ).astype(BF16)
    back_other, grad_out_other = lax.optimization_barrier((back_other, grad_out_other))
    grad_out_got = swap(grad_out_other, 1)
    back_got = swap(back_other, 2)
    grad_in_got = swap(grad_in(pre_grad[..., quarter:]).astype(BF16), 1)

    back_own = jnp.einsum("ecf,edf->ecd", pre_grad[:, :cap], proj_in, preferred_element_type=F32)
    slot_back = (back_own + back_got.astype(F32)).astype(BF16).reshape(slots, width)
    outgoing = jnp.dot(slot_pick.T, slot_back, preferred_element_type=F32).astype(BF16)
    outgoing, grad_out_got = lax.optimization_barrier((outgoing, grad_out_got))
    returned = exchange(outgoing, owners)

    w_out_grad = (grad_out(hidden[..., :quarter]) + grad_out_got.astype(F32)).astype(BF16)
    returned, grad_in_got = lax.optimization_barrier((returned, grad_in_got))
    w_in_grad = (grad_in(pre_grad[..., :quarter]) + grad_in_got.astype(F32)).astype(BF16)
    token_grad = jnp.dot(send_pick.T, returned, preferred_element_type=F32).astype(BF16)
    gate_grad = gate_part[:, :cap] + gate_got
    return token_grad[None], gate_grad[None], w_in_grad, w_out_grad


def solution(mesh):
    return jax.shard_map(
        shards,
        mesh=mesh,
        in_specs=(
            P("dp", "expert", None),
            P("dp", "expert"),
            P("dp", "expert", None),
            P("dp", "expert", None),
            P("dp", "expert", None, None),
            P("expert", None, "dp"),
            P("expert", "dp", None),
        ),
        out_specs=(
            P("dp", "expert", None),
            P("dp", "expert", None),
            P("expert", None, "dp"),
            P("expert", "dp", None),
        ),
        check_vma=False,
    )
```
